32 devices in a mesh: groups: 2 (over y), vocab: 4 (over z), dp: 2 (over x), rep: 2 (over core).
Axes of the slice: x: 2, y: 2, z: 4, core: 2. Of those that a mesh axis runs over, the one named last changes fastest.
Arguments:
- hidden: bfloat16 [512, 4608], P(('groups', 'dp', 'rep')), parts along dimension 0, may hold values from -6 to 6
- cotangent: bfloat16 [512, 4608], P(('groups', 'dp', 'rep')), parts along dimension 0, may hold values from -0.09375 to 0.09375
- table: bfloat16 [1024, 4608], P('vocab', ('dp', 'rep')), may hold values from -0.25 to 0.25
- token_ids: int32 [512], P('groups'), parts along dimension 0, may hold values from 0 to 1023
- target_ids: int32 [512], P('groups'), parts along dimension 0, may hold values from 0 to 1023
- row_counts: int32 [8], P('groups'), parts along dimension 0, may hold values from 16 to 64
Outputs:
- hidden_grad: bfloat16 [512, 4608], P('groups', ('dp', 'rep')), parts along dimension 0
- table_grad: bfloat16 [2048, 4608], P(('groups', 'vocab'), ('dp', 'rep')), parts along dimension 0
The draws below stay inside these ranges and needn't reach their ends.
There are 2 independent parts, one for each index of `groups`. The reference program is written for one: setup_inputs(seed, part) draws one part's arguments, and reference() takes and returns one part's arrays. A program takes and returns all parts, laid end to end along the dimension named above; an argument that names none is the same for every part. Nothing has to cross between parts.
All inputs are finite; a program needn't handle non-finite values.
Results may differ from the reference program's by a relative error of at most 0.0049.
Values may be sent and summed in bfloat16 or wider, within the bound.
A program may use at most 64 MiB of HBM per device.

```python
import math
import jax
import jax.numpy as jnp
import numpy as np
from jax import lax

D = 4608
CAP = 30
ROW_LEN = 64
VOCAB = 1024
TOKENS = 256
ROWS = 4


def plant(array, own_key, smallest, top_value):
    longest = array.shape.index(max(array.shape))
    spots = []
    for shift in (0, 1):
        where = [jax.random.randint(jax.random.fold_in(own_key, axis), (), 0, length) for axis, length in enumerate(array.shape)]
        where[longest] = (where[longest] + shift) % array.shape[longest]
        spots.append(tuple(where))
    return array.at[spots[0]].set(smallest).at[spots[1]].set(top_value)


def steps_of(own_key, extent, shards, least, high):
    level = 1.0
    for dim, parts in shards:
        heights = jax.random.uniform(jax.random.fold_in(jax.random.fold_in(own_key, 6), dim), (parts,), jnp.float32, least / len(shards), high / len(shards))
        level = level * jnp.repeat(jnp.exp(heights), extent[dim] // parts).reshape((-1,) + (1,) * (len(extent) - 1 - dim))
    return level


def rank_bounds(number_of, slope):
    portions = [(1 << 20) // math.isqrt(rank ** slope) + 1 for rank in range(1, number_of + 1)]
    scale = 1 + sum(portions) // (1 << 30)
    return np.cumsum(np.array([max(1, weight // scale) for weight in portions]))


def ranked_ids(key, dims, number_of, slope):
    listing = rank_bounds(number_of, slope)
    ticket = jax.random.randint(jax.random.fold_in(key, 1), dims, 0, int(listing[number_of - 1]))
    standing = jnp.searchsorted(jnp.asarray(listing, jnp.int32), ticket, side="right")
    return jax.random.permutation(jax.random.fold_in(key, 2), number_of)[standing].astype(jnp.int32)


def gaussian(own_key, dims, width, reach, shards=(), held_as=jnp.bfloat16):
    array = width * jax.random.normal(own_key, dims, jnp.float32)
    if shards:
        array = array * steps_of(own_key, dims, shards, -0.22, 0.18)
    return jnp.clip(array, -reach, reach).astype(held_as)


def setup_inputs(seed: int = 0, part: int = 0) -> dict:
    streams_of = jax.random.split(jax.random.key(seed), 7)
    own_keys = jax.random.split(jax.random.fold_in(streams_of[6], part), 7)
    return {
        "hidden": gaussian(own_keys[0], (TOKENS, D), 1.0, 6.0, ((0, 4),)),
        "cotangent": gaussian(own_keys[1], (TOKENS, D), D ** -0.5, 0.09375, ((0, 4),)),
        "table": gaussian(streams_of[2], (VOCAB, D), (D // 9) ** -0.5, 0.25, ((0, 4), (1, 4))),
        "token_ids": plant(ranked_ids(own_keys[3], (TOKENS,), VOCAB, 2), jax.random.fold_in(own_keys[3], 3), 0, VOCAB - 1).astype(jnp.int32),
        "target_ids": plant(ranked_ids(own_keys[4], (TOKENS,), VOCAB, 2), jax.random.fold_in(own_keys[4], 3), 0, VOCAB - 1).astype(jnp.int32),
        "row_counts": plant(jax.random.randint(own_keys[5], (ROWS,), ROW_LEN // 4, ROW_LEN + 1), jax.random.fold_in(own_keys[5], 1), ROW_LEN // 4, ROW_LEN).astype(jnp.int32),
    }


def token_weights(row_counts):
    slots = jnp.arange(ROW_LEN, dtype=jnp.int32)[None, :]
    counts = row_counts[:, None]
    scale = ROW_LEN / counts.astype(jnp.float32)
    return jnp.where(slots < counts, scale, jnp.float32(0.0)).reshape(-1).astype(jnp.float32)

def reference(hidden, cotangent, table, token_ids, target_ids, row_counts):
    weight = token_weights(row_counts)
    raw = lax.dot_general(hidden, table, (((1,), (1,)), ((), ())), preferred_element_type=jnp.float32)
    squash = jnp.tanh(raw / CAP)
    expo = jnp.exp(CAP * squash)
    total = lax.optimization_barrier(jnp.sum(expo, axis=1))
    vocab_rows = jnp.arange(VOCAB, dtype=jnp.int32)
    hit = (target_ids[:, None] == vocab_rows[None, :]).astype(jnp.float32)
    logit_grad = (weight[:, None] * (expo / total[:, None] - hit) * (1.0 - squash * squash)).astype(jnp.bfloat16)
    hidden_grad = jnp.dot(logit_grad, table, preferred_element_type=jnp.float32).astype(jnp.bfloat16)
    head = lax.dot_general(logit_grad, hidden, (((0,), (0,)), ((), ())), preferred_element_type=jnp.float32)
    embed = jnp.zeros((VOCAB, D), jnp.float32).at[token_ids].add(cotangent.astype(jnp.float32))
    table_grad = (head + math.sqrt(D) * embed).astype(jnp.bfloat16)
    return (hidden_grad, table_grad)
```

```python
import math

import jax
import jax.numpy as jnp
from jax import lax
from jax.experimental import pallas as pl
from jax.experimental.pallas import tpu as pltpu
from jax.sharding import PartitionSpec as P

D = 4608
CAP = 30
ROW_LEN = 64


def token_weights(row_counts):
    slots = jnp.arange(ROW_LEN, dtype=jnp.int32)[None, :]
    counts = row_counts[:, None]
    scale = ROW_LEN / counts.astype(jnp.float32)
    return jnp.where(slots < counts, scale, jnp.float32(0.0)).reshape(-1)


def plain(hidden, cotangent, table, token_ids, target_ids, row_counts):
    h_cols, g_cols = (
        lax.all_to_all(hidden, ("dp", "rep"), split_axis=1, concat_axis=0, tiled=True),
        lax.all_to_all(cotangent, ("dp", "rep"), split_axis=1, concat_axis=0, tiled=True),
    )
    block = table.shape[0]
    parts = lax.axis_size(("dp", "rep"))
    base = lax.axis_index("vocab") * block
    weight = token_weights(row_counts)
    span = block // parts
    raw = lax.psum_scatter(
        lax.dot_general(
            table, h_cols, (((1,), (1,)), ((), ())), preferred_element_type=jnp.float32
        ),
        ("dp", "rep"),
        scatter_dimension=0,
        tiled=True,
    )
    first = base + lax.axis_index(("dp", "rep")) * span
    squash = jnp.tanh(raw / CAP)
    expo = jnp.exp(CAP * squash)
    total = lax.psum(jnp.sum(expo, axis=0), ("vocab", "dp", "rep"))
    row_ids = first + jnp.arange(span, dtype=jnp.int32)
    hit = (target_ids[None, :] == row_ids[:, None]).astype(jnp.float32)
    grad = (weight[None, :] * (expo / total[None, :] - hit) * (1.0 - squash * squash)).astype(
        jnp.bfloat16
    )
    grads = lax.all_gather(grad, ("dp", "rep"), axis=0, tiled=True)
    head = jnp.dot(grads, h_cols, preferred_element_type=jnp.float32)
    partial_sum = lax.dot_general(
        grads, table, (((0,), (0,)), ((), ())), preferred_element_type=jnp.float32
    )
    block_ids = base + jnp.arange(block, dtype=jnp.int32)
    one_hot = (token_ids[:, None] == block_ids[None, :]).astype(jnp.bfloat16)
    embed = lax.dot_general(
        one_hot, g_cols, (((0,), (0,)), ((), ())), preferred_element_type=jnp.float32
    )
    table_grad = (head + math.sqrt(D) * embed).astype(jnp.bfloat16)
    hidden_grad = lax.psum(partial_sum, "vocab").astype(jnp.bfloat16)
    return (hidden_grad, table_grad)


MESH = pl.DeviceIdType.MESH
TILE = 384


def kernel(
    hid, cot, tab, tok, tgt, cnt,
    hid_out, tab_out,
    tall, hcols, gcols, part, rawin, tot, gall, tcol,
    loc_sem, h_snd, h_rcv, c_snd, c_rcv, tz_snd, tz_rcv, ty_snd, ty_rcv,
    p_snd, p_rcv, s_snd, s_rcv, g_snd, g_rcv, f_snd, f_rcv,
):
    y, z = lax.axis_index("groups"), lax.axis_index("vocab")
    x, c = lax.axis_index("dp"), lax.axis_index("rep")
    p = 2 * x + c
    cols = tab.shape[1]
    block = tab.shape[0]
    half = block // 2
    near = {1: (x, 1 - c), 2: (1 - x, c), 3: (1 - x, 1 - c)}
    near_id = {k: {"dp": a, "rep": b} for k, (a, b) in near.items()}
    place = {0: p, **{k: 2 * a + b for k, (a, b) in near.items()}}
    up_id = {d: {"vocab": lax.rem(z + d, 4)} for d in (1, 2, 3)}
    down = {d: lax.rem(z + 4 - d, 4) for d in (1, 2, 3)}
    twin = {"groups": 1 - y}

    def remote(src, dst, snd, rcv, to):
        return pltpu.make_async_remote_copy(
            src_ref=src, dst_ref=dst, send_sem=snd, recv_sem=rcv, device_id=to, device_id_type=MESH
        )

    def my_cols(q):
        return pl.ds(pl.multiple_of(q * cols, 128), cols)

    own = [
        pltpu.make_async_copy(hid.at[:, my_cols(p)], hcols.at[p], loc_sem.at[0]),
        pltpu.make_async_copy(tab, tall.at[z], loc_sem.at[1]),
        pltpu.make_async_copy(cot.at[:, my_cols(p)], gcols.at[p], loc_sem.at[2]),
    ]
    for copy in own:
        copy.start()

    barrier = pltpu.get_barrier_semaphore()
    for to in (*near_id.values(), *up_id.values(), twin):
        pl.semaphore_signal(barrier, inc=1, device_id=to, device_id_type=MESH)
    pl.semaphore_wait(barrier, 7)

    send_h = {
        k: remote(hid.at[:, my_cols(place[k])], hcols.at[p], h_snd.at[k], h_rcv.at[k], near_id[k])
        for k in (2, 3, 1)
    }
    for copy in send_h.values():
        copy.start()
    mine = pl.ds(pl.multiple_of(half * y, half), half)
    send_t = {
        d: remote(tab.at[mine], tall.at[z, mine], tz_snd.at[d], tz_rcv.at[d], up_id[d])
        for d in (1, 3, 2)
    }
    for copy in send_t.values():
        copy.start()

    ids = jnp.broadcast_to(tgt[...].astype(jnp.float32), (128, tgt.shape[1]))
    tcol[...] = ids.T

    for copy in own:
        copy.wait()
    send_p = {}
    for k in (0, 1, 2, 3):
        if k:
            send_h[k].wait_recv()
        part[k] = lax.dot_general(
            hcols[place[k]], tall[z], (((1,), (1,)), ((), ())), preferred_element_type=jnp.float32
        )
        if k:
            send_p[k] = remote(part.at[k], rawin.at[k], p_snd.at[k], p_rcv.at[k], near_id[k])
            send_p[k].start()
    send_c = {
        k: remote(cot.at[:, my_cols(place[k])], gcols.at[p], c_snd.at[k], c_rcv.at[k], near_id[k])
        for k in (2, 3, 1)
    }
    for copy in send_c.values():
        copy.start()

    raw = part[0]
    for k in (1, 2, 3):
        send_p[k].wait_recv()
        raw = raw + rawin[k]
    squash = jnp.tanh(raw / CAP)
    expo = jnp.exp(CAP * squash)
    line = jnp.broadcast_to(jnp.sum(expo, axis=1, keepdims=True), (ROW_LEN, 128))
    tot[0] = jnp.concatenate([line, line], axis=0).T[:8]
    send_s = {d: remote(tot.at[0], tot.at[d], s_snd.at[d], s_rcv.at[d], up_id[d]) for d in (1, 2, 3)}
    for copy in send_s.values():
        copy.start()
    target = tcol[pl.ds(pl.multiple_of(ROW_LEN * p, ROW_LEN), ROW_LEN), :]
    target = jnp.concatenate([target] * (block // 128), axis=1)
    row_ids = (z * block + lax.broadcasted_iota(jnp.int32, (ROW_LEN, block), 1)).astype(jnp.float32)
    hit = (target == row_ids).astype(jnp.float32)
    count = jnp.full((ROW_LEN, block), cnt[p], jnp.int32)
    slot = lax.broadcasted_iota(jnp.int32, (ROW_LEN, block), 0)
    weight = jnp.where(slot < count, ROW_LEN / count.astype(jnp.float32), 0.0)
    slope = 1.0 - squash * squash
    for copy in send_s.values():
        copy.wait_recv()
    whole = tot[0] + tot[1] + tot[2] + tot[3]
    whole = jnp.broadcast_to(whole[:1], (128, 128)).T[:ROW_LEN]
    whole = jnp.concatenate([whole] * (block // 128), axis=1)
    gall[z, p] = (weight * (expo / whole - hit) * slope).astype(jnp.bfloat16)

    send_g = {d: remote(gall.at[z, p], gall.at[z, p], g_snd.at[d], g_rcv.at[d], up_id[d]) for d in (1, 2, 3)}
    for copy in send_g.values():
        copy.start()
    send_f = {}

    def hand_on(d, row):
        for k in (2, 3, 1):
            piece = gall.at[row, p]
            send_f[d, k] = remote(piece, piece, f_snd.at[d, k], f_rcv.at[d, k], near_id[k])
            send_f[d, k].start()

    hand_on(0, z)
    send_y = {}
    for d in (1, 3, 2):
        send_g[d].wait_recv()
        hand_on(d, down[d])
        send_t[d].wait_recv()
        piece = tall.at[down[d], mine]
        send_y[d] = remote(piece, piece, ty_snd.at[d], ty_rcv.at[d], twin)
        send_y[d].start()

    for k in (2, 3, 1):
        send_c[k].wait_recv()
        send_f[0, k].wait_recv()
    tokens = tok.shape[1]
    vocab_ids = z * block + lax.broadcasted_iota(jnp.int32, (block, tokens), 0)
    one_hot = (jnp.broadcast_to(tok[...], (block, tokens)) == vocab_ids).astype(jnp.float32)
    one_hot = one_hot.astype(jnp.bfloat16)
    grads = gall[z].reshape(tokens, block)

    @pl.loop(0, cols // TILE)
    def _(j):
        at = pl.ds(pl.multiple_of(j * TILE, 128), TILE)
        head = lax.dot_general(
            grads, hcols[:, :, at].reshape(tokens, TILE), (((0,), (0,)), ((), ())),
            preferred_element_type=jnp.float32,
        )
        embed = jnp.dot(
            one_hot, gcols[:, :, at].reshape(tokens, TILE), preferred_element_type=jnp.float32
        )
        tab_out[:, at] = (head + math.sqrt(D) * embed).astype(jnp.bfloat16)

    for d in (1, 3, 2):
        send_y[d].wait_recv()
        for k in (2, 3, 1):
            send_f[d, k].wait_recv()

    @pl.loop(0, cols // TILE)
    def _(j):
        at = pl.ds(pl.multiple_of(j * TILE, 128), TILE)
        total = jnp.zeros((tokens, TILE), jnp.float32)
        for row in range(4):
            total = total + jnp.dot(
                gall[row].reshape(tokens, block), tall[row, :, at], preferred_element_type=jnp.float32
            )
        hid_out[:, at] = total.astype(jnp.bfloat16)

    for group in (send_h, send_t, send_p, send_c, send_s, send_g, send_f, send_y):
        for copy in group.values():
            copy.wait_send()


def shards(hidden, cotangent, table, token_ids, target_ids, row_counts):
    block, cols = table.shape
    rows = hidden.shape[0]
    tokens = token_ids.shape[0]
    vmem = pl.BlockSpec(memory_space=pltpu.VMEM)
    hbm = pl.BlockSpec(memory_space=pl.ANY)
    dma = pltpu.SemaphoreType.DMA
    return pl.pallas_call(
        kernel,
        out_shape=(
            jax.ShapeDtypeStruct((tokens, cols), jnp.bfloat16),
            jax.ShapeDtypeStruct((block, cols), jnp.bfloat16),
        ),
        in_specs=[hbm, hbm, hbm, vmem, vmem, pl.BlockSpec(memory_space=pltpu.SMEM)],
        out_specs=(vmem, vmem),
        scratch_shapes=[
            pltpu.VMEM((4, block, cols), jnp.bfloat16),
            pltpu.VMEM((4, rows, cols), jnp.bfloat16),
            pltpu.VMEM((4, rows, cols), jnp.bfloat16),
            pltpu.VMEM((4, rows, block), jnp.float32),
            pltpu.VMEM((4, rows, block), jnp.float32),
            pltpu.VMEM((4, 8, 128), jnp.float32),
            pltpu.VMEM((4, 4, rows, block), jnp.bfloat16),
            pltpu.VMEM((tokens, 128), jnp.float32),
            dma((3,)),
            *[dma((4,))] * 14,
            dma((4, 4)),
            dma((4, 4)),
        ],
        compiler_params=pltpu.CompilerParams(
            collective_id=0, has_side_effects=True, vmem_limit_bytes=40 * 1024 * 1024
        ),
        cost_estimate=pl.CostEstimate(flops=1200000000, bytes_accessed=6000000, transcendentals=40000),
    )(hidden, cotangent, table, token_ids[None, :], target_ids[None, :], row_counts)


def solution(mesh):
    sizes = tuple(mesh.shape[axis] for axis in ("groups", "vocab", "dp", "rep"))

    def part(hidden, cotangent, table, token_ids, target_ids, row_counts):
        block, cols = table.shape
        fits = (
            sizes == (2, 4, 2, 2)
            and hidden.shape[0] == ROW_LEN
            and cols % TILE == 0
            and block == 256
            and token_ids.shape[0] == 256
        )
        run = shards if fits else plain
        return run(hidden, cotangent, table, token_ids, target_ids, row_counts)

    in_specs = (
        P(("groups", "dp", "rep"), None),
        P(("groups", "dp", "rep"), None),
        P("vocab", ("dp", "rep")),
        P("groups"),
        P("groups"),
        P("groups"),
    )
    out_specs = (P("groups", ("dp", "rep")), P(("groups", "vocab"), ("dp", "rep")))
    return jax.shard_map(part, mesh=mesh, in_specs=in_specs, out_specs=out_specs, check_vma=False)
```

```python
import math

import jax
import jax.numpy as jnp
from jax import lax
from jax.experimental import pallas as pl
from jax.experimental.pallas import tpu as pltpu
from jax.sharding import PartitionSpec as P

D = 4608
CAP = 30
ROW_LEN = 64


def token_weights(row_counts):
    slots = jnp.arange(ROW_LEN, dtype=jnp.int32)[None, :]
    counts = row_counts[:, None]
    scale = ROW_LEN / counts.astype(jnp.float32)
    return jnp.where(slots < counts, scale, jnp.float32(0.0)).reshape(-1)


def plain(hidden, cotangent, table, token_ids, target_ids, row_counts):
    h_cols, g_cols = (
        lax.all_to_all(hidden, ("dp", "rep"), split_axis=1, concat_axis=0, tiled=True),
        lax.all_to_all(cotangent, ("dp", "rep"), split_axis=1, concat_axis=0, tiled=True),
    )
    block = table.shape[0]
    parts = lax.axis_size(("dp", "rep"))
    base = lax.axis_index("vocab") * block
    weight = token_weights(row_counts)
    span = block // parts
    raw = lax.psum_scatter(
        lax.dot_general(
            table, h_cols, (((1,), (1,)), ((), ())), preferred_element_type=jnp.float32
        ),
        ("dp", "rep"),
        scatter_dimension=0,
        tiled=True,
    )
    first = base + lax.axis_index(("dp", "rep")) * span
    squash = jnp.tanh(raw / CAP)
    expo = jnp.exp(CAP * squash)
    total = lax.psum(jnp.sum(expo, axis=0), ("vocab", "dp", "rep"))
    row_ids = first + jnp.arange(span, dtype=jnp.int32)
    hit = (target_ids[None, :] == row_ids[:, None]).astype(jnp.float32)
    grad = (weight[None, :] * (expo / total[None, :] - hit) * (1.0 - squash * squash)).astype(
        jnp.bfloat16
    )
    grads = lax.all_gather(grad, ("dp", "rep"), axis=0, tiled=True)
    head = jnp.dot(grads, h_cols, preferred_element_type=jnp.float32)
    partial_sum = lax.dot_general(
        grads, table, (((0,), (0,)), ((), ())), preferred_element_type=jnp.float32
    )
    block_ids = base + jnp.arange(block, dtype=jnp.int32)
    one_hot = (token_ids[:, None] == block_ids[None, :]).astype(jnp.bfloat16)
    embed = lax.dot_general(
        one_hot, g_cols, (((0,), (0,)), ((), ())), preferred_element_type=jnp.float32
    )
    table_grad = (head + math.sqrt(D) * embed).astype(jnp.bfloat16)
    hidden_grad = lax.psum(partial_sum, "vocab").astype(jnp.bfloat16)
    return (hidden_grad, table_grad)


MESH = pl.DeviceIdType.MESH
TILE = 384


def kernel(
    hid, cot, tab, tok, tgt, cnt,
    hid_out, tab_out,
    tall, hcols, gcols, part, rawin, tot, gall, tcol,
    loc_sem, h_snd, h_rcv, c_snd, c_rcv, tz_snd, tz_rcv, ty_snd, ty_rcv,
    p_snd, p_rcv, s_snd, s_rcv, g_snd, g_rcv, f_snd, f_rcv,
):
    y, z = lax.axis_index("groups"), lax.axis_index("vocab")
    x, c = lax.axis_index("dp"), lax.axis_index("rep")
    p = 2 * x + c
    cols = tab.shape[1]
    block = tab.shape[0]
    half = block // 2
    near = {1: (x, 1 - c), 2: (1 - x, c), 3: (1 - x, 1 - c)}
    near_id = {k: {"dp": a, "rep": b} for k, (a, b) in near.items()}
    place = {0: p, **{k: 2 * a + b for k, (a, b) in near.items()}}
    up_id = {d: {"vocab": lax.rem(z + d, 4)} for d in (1, 2, 3)}
    down = {d: lax.rem(z + 4 - d, 4) for d in (1, 2, 3)}
    twin = {"groups": 1 - y}

    def remote(src, dst, snd, rcv, to):
        return pltpu.make_async_remote_copy(
            src_ref=src, dst_ref=dst, send_sem=snd, recv_sem=rcv, device_id=to, device_id_type=MESH
        )

    def my_cols(q):
        return pl.ds(pl.multiple_of(q * cols, 128), cols)

    own = [
        pltpu.make_async_copy(hid.at[:, my_cols(p)], hcols.at[p], loc_sem.at[0]),
        pltpu.make_async_copy(tab, tall.at[z], loc_sem.at[1]),
        pltpu.make_async_copy(cot.at[:, my_cols(p)], gcols.at[p], loc_sem.at[2]),
    ]
    for copy in own:
        copy.start()

    barrier = pltpu.get_barrier_semaphore()
    for to in (*near_id.values(), *up_id.values(), twin):
        pl.semaphore_signal(barrier, inc=1, device_id=to, device_id_type=MESH)
    pl.semaphore_wait(barrier, 7)

    send_h = {
        k: remote(hid.at[:, my_cols(place[k])], hcols.at[p], h_snd.at[k], h_rcv.at[k], near_id[k])
        for k in (2, 3, 1)
    }
    for copy in send_h.values():
        copy.start()
    mine = pl.ds(pl.multiple_of(half * y, half), half)

    def relay(s, way):
        row = z - way * (s - 1)
        src = tab.at[mine] if s == 1 else tall.at[row, mine]
        lane = s if way == 1 else s + 4
        copy = remote(src, tall.at[row, mine], tz_snd.at[lane], tz_rcv.at[lane], {"vocab": z + way})
        on = (z < 3) & (row >= 0) if way == 1 else (z > 0) & (row <= 3)
        return on, copy

    def landed(s, way):
        row = z - way * s
        piece = tall.at[row, mine]
        lane = s if way == 1 else s + 4
        came = remote(piece, piece, tz_snd.at[lane], tz_rcv.at[lane], {"vocab": z + way})
        over = remote(piece, piece, ty_snd.at[lane], ty_rcv.at[lane], twin)
        on = row >= 0 if way == 1 else row <= 3
        return on, came, over

    def pass_on(s):
        for way in (1, -1):
            on, came, over = landed(s, way)

            @pl.when(on)
            def _():
                came.wait_recv()
                over.start()

            if s < 3:
                on, copy = relay(s + 1, way)

                @pl.when(on)
                def _():
                    copy.start()

    for way in (1, -1):
        on, copy = relay(1, way)

        @pl.when(on)
        def _():
            copy.start()

    ids = jnp.broadcast_to(tgt[...].astype(jnp.float32), (128, tgt.shape[1]))
    tcol[...] = ids.T

    for copy in own:
        copy.wait()
    send_p = {}
    for k in (0, 1, 2, 3):
        if k:
            send_h[k].wait_recv()
        part[k] = lax.dot_general(
            hcols[place[k]], tall[z], (((1,), (1,)), ((), ())), preferred_element_type=jnp.float32
        )
        if k:
            send_p[k] = remote(part.at[k], rawin.at[k], p_snd.at[k], p_rcv.at[k], near_id[k])
            send_p[k].start()
    send_c = {
        k: remote(cot.at[:, my_cols(place[k])], gcols.at[p], c_snd.at[k], c_rcv.at[k], near_id[k])
        for k in (2, 3, 1)
    }
    for copy in send_c.values():
        copy.start()
    pass_on(1)

    raw = part[0]
    for k in (1, 2, 3):
        send_p[k].wait_recv()
        raw = raw + rawin[k]
    squash = jnp.tanh(raw / CAP)
    expo = jnp.exp(CAP * squash)
    line = jnp.broadcast_to(jnp.sum(expo, axis=1, keepdims=True), (ROW_LEN, 128))
    tot[0] = jnp.concatenate([line, line], axis=0).T[:8]
    send_s = {d: remote(tot.at[0], tot.at[d], s_snd.at[d], s_rcv.at[d], up_id[d]) for d in (1, 2, 3)}
    for copy in send_s.values():
        copy.start()
    target = tcol[pl.ds(pl.multiple_of(ROW_LEN * p, ROW_LEN), ROW_LEN), :]
    target = jnp.concatenate([target] * (block // 128), axis=1)
    row_ids = (z * block + lax.broadcasted_iota(jnp.int32, (ROW_LEN, block), 1)).astype(jnp.float32)
    hit = (target == row_ids).astype(jnp.float32)
    count = jnp.full((ROW_LEN, block), cnt[p], jnp.int32)
    slot = lax.broadcasted_iota(jnp.int32, (ROW_LEN, block), 0)
    weight = jnp.where(slot < count, ROW_LEN / count.astype(jnp.float32), 0.0)
    slope = 1.0 - squash * squash
    for copy in send_s.values():
        copy.wait_recv()
    whole = tot[0] + tot[1] + tot[2] + tot[3]
    whole = jnp.broadcast_to(whole[:1], (128, 128)).T[:ROW_LEN]
    whole = jnp.concatenate([whole] * (block // 128), axis=1)
    gall[z, p] = (weight * (expo / whole - hit) * slope).astype(jnp.bfloat16)

    send_g = {d: remote(gall.at[z, p], gall.at[z, p], g_snd.at[d], g_rcv.at[d], up_id[d]) for d in (1, 2, 3)}
    for copy in send_g.values():
        copy.start()
    send_f = {}

    def hand_on(d, row, k):
        piece = gall.at[row, place[2] if k == 3 else p]
        to = near_id[1 if k == 3 else k]
        send_f[d, k] = remote(piece, piece, f_snd.at[d, k], f_rcv.at[d, k], to)
        send_f[d, k].start()

    hand_on(0, z, 2)
    hand_on(0, z, 1)
    pass_on(2)
    for d in (1, 3, 2):
        send_g[d].wait_recv()
        hand_on(d, down[d], 2)
        hand_on(d, down[d], 1)
    for d in (0, 1, 3, 2):
        send_f[d, 2].wait_recv()
        hand_on(d, down[d] if d else z, 3)
    pass_on(3)

    for k in (2, 3, 1):
        send_c[k].wait_recv()
    for k in (1, 3):
        send_f[0, k].wait_recv()
    tokens = tok.shape[1]
    vocab_ids = z * block + lax.broadcasted_iota(jnp.int32, (block, tokens), 0)
    one_hot = (jnp.broadcast_to(tok[...], (block, tokens)) == vocab_ids).astype(jnp.float32)
    one_hot = one_hot.astype(jnp.bfloat16)
    grads = gall[z].reshape(tokens, block)

    @pl.loop(0, cols // TILE)
    def _(j):
        at = pl.ds(pl.multiple_of(j * TILE, 128), TILE)
        head = lax.dot_general(
            grads, hcols[:, :, at].reshape(tokens, TILE), (((0,), (0,)), ((), ())),
            preferred_element_type=jnp.float32,
        )
        embed = jnp.dot(
            one_hot, gcols[:, :, at].reshape(tokens, TILE), preferred_element_type=jnp.float32
        )
        tab_out[:, at] = (head + math.sqrt(D) * embed).astype(jnp.bfloat16)

    for d in (1, 3, 2):
        for k in (1, 3):
            send_f[d, k].wait_recv()
    for s in (1, 2, 3):
        for way in (1, -1):
            on, _, over = landed(s, way)

            @pl.when(on)
            def _():
                over.wait()

            on, copy = relay(s, way)

            @pl.when(on)
            def _():
                copy.wait_send()

    @pl.loop(0, cols // TILE)
    def _(j):
        at = pl.ds(pl.multiple_of(j * TILE, 128), TILE)
        total = jnp.zeros((tokens, TILE), jnp.float32)
        for row in range(4):
            total = total + jnp.dot(
                gall[row].reshape(tokens, block), tall[row, :, at], preferred_element_type=jnp.float32
            )
        hid_out[:, at] = total.astype(jnp.bfloat16)

    for group in (send_h, send_p, send_c, send_s, send_g, send_f):
        for copy in group.values():
            copy.wait_send()


def shards(hidden, cotangent, table, token_ids, target_ids, row_counts):
    block, cols = table.shape
    rows = hidden.shape[0]
    tokens = token_ids.shape[0]
    vmem = pl.BlockSpec(memory_space=pltpu.VMEM)
    hbm = pl.BlockSpec(memory_space=pl.ANY)
    dma = pltpu.SemaphoreType.DMA
    return pl.pallas_call(
        kernel,
        out_shape=(
            jax.ShapeDtypeStruct((tokens, cols), jnp.bfloat16),
            jax.ShapeDtypeStruct((block, cols), jnp.bfloat16),
        ),
        in_specs=[hbm, hbm, hbm, vmem, vmem, pl.BlockSpec(memory_space=pltpu.SMEM)],
        out_specs=(vmem, vmem),
        scratch_shapes=[
            pltpu.VMEM((4, block, cols), jnp.bfloat16),
            pltpu.VMEM((4, rows, cols), jnp.bfloat16),
            pltpu.VMEM((4, rows, cols), jnp.bfloat16),
            pltpu.VMEM((4, rows, block), jnp.float32),
            pltpu.VMEM((4, rows, block), jnp.float32),
            pltpu.VMEM((4, 8, 128), jnp.float32),
            pltpu.VMEM((4, 4, rows, block), jnp.bfloat16),
            pltpu.VMEM((tokens, 128), jnp.float32),
            dma((3,)),
            *[dma((4,))] * 4,
            *[dma((8,))] * 4,
            *[dma((4,))] * 6,
            dma((4, 4)),
            dma((4, 4)),
        ],
        compiler_params=pltpu.CompilerParams(
            collective_id=0, has_side_effects=True, vmem_limit_bytes=60 * 1024 * 1024
        ),
        cost_estimate=pl.CostEstimate(flops=1200000000, bytes_accessed=6000000, transcendentals=40000),
    )(hidden, cotangent, table, token_ids[None, :], target_ids[None, :], row_counts)


def solution(mesh):
    sizes = tuple(mesh.shape[axis] for axis in ("groups", "vocab", "dp", "rep"))

    def part(hidden, cotangent, table, token_ids, target_ids, row_counts):
        block, cols = table.shape
        fits = (
            sizes == (2, 4, 2, 2)
            and hidden.shape[0] == ROW_LEN
            and cols % TILE == 0
            and block == 256
            and token_ids.shape[0] == 256
        )
        run = shards if fits else plain
        return run(hidden, cotangent, table, token_ids, target_ids, row_counts)

    in_specs = (
        P(("groups", "dp", "rep"), None),
        P(("groups", "dp", "rep"), None),
        P("vocab", ("dp", "rep")),
        P("groups"),
        P("groups"),
        P("groups"),
    )
    out_specs = (P("groups", ("dp", "rep")), P(("groups", "vocab"), ("dp", "rep")))
    return jax.shard_map(part, mesh=mesh, in_specs=in_specs, out_specs=out_specs, check_vma=False)
```

```python
import math

import jax
import jax.numpy as jnp
from jax import lax
from jax.experimental import pallas as pl
from jax.experimental.pallas import tpu as pltpu
from jax.sharding import PartitionSpec as P

D = 4608
CAP = 30
ROW_LEN = 64


def token_weights(row_counts):
    slots = jnp.arange(ROW_LEN, dtype=jnp.int32)[None, :]
    counts = row_counts[:, None]
    scale = ROW_LEN / counts.astype(jnp.float32)
    return jnp.where(slots < counts, scale, jnp.float32(0.0)).reshape(-1)


def plain(hidden, cotangent, table, token_ids, target_ids, row_counts):
    h_cols, g_cols = (
        lax.all_to_all(hidden, ("dp", "rep"), split_axis=1, concat_axis=0, tiled=True),
        lax.all_to_all(cotangent, ("dp", "rep"), split_axis=1, concat_axis=0, tiled=True),
    )
    block = table.shape[0]
    parts = lax.axis_size(("dp", "rep"))
    base = lax.axis_index("vocab") * block
    weight = token_weights(row_counts)
    span = block // parts
    raw = lax.psum_scatter(
        lax.dot_general(
            table, h_cols, (((1,), (1,)), ((), ())), preferred_element_type=jnp.float32
        ),
        ("dp", "rep"),
        scatter_dimension=0,
        tiled=True,
    )
    first = base + lax.axis_index(("dp", "rep")) * span
    squash = jnp.tanh(raw / CAP)
    expo = jnp.exp(CAP * squash)
    total = lax.psum(jnp.sum(expo, axis=0), ("vocab", "dp", "rep"))
    row_ids = first + jnp.arange(span, dtype=jnp.int32)
    hit = (target_ids[None, :] == row_ids[:, None]).astype(jnp.float32)
    grad = (weight[None, :] * (expo / total[None, :] - hit) * (1.0 - squash * squash)).astype(
        jnp.bfloat16
    )
    grads = lax.all_gather(grad, ("dp", "rep"), axis=0, tiled=True)
    head = jnp.dot(grads, h_cols, preferred_element_type=jnp.float32)
    partial_sum = lax.dot_general(
        grads, table, (((0,), (0,)), ((), ())), preferred_element_type=jnp.float32
    )
    block_ids = base + jnp.arange(block, dtype=jnp.int32)
    one_hot = (token_ids[:, None] == block_ids[None, :]).astype(jnp.bfloat16)
    embed = lax.dot_general(
        one_hot, g_cols, (((0,), (0,)), ((), ())), preferred_element_type=jnp.float32
    )
    table_grad = (head + math.sqrt(D) * embed).astype(jnp.bfloat16)
    hidden_grad = lax.psum(partial_sum, "vocab").astype(jnp.bfloat16)
    return (hidden_grad, table_grad)


MESH = pl.DeviceIdType.MESH
TILE = 384


def kernel(
    hid, cot, tab, tok, tgt, cnt,
    hid_out, tab_out,
    tall, hcols, gcols, part, rawin, tot, gall, tcol,
    loc_sem, h_snd, h_rcv, c_snd, c_rcv, tz_snd, tz_rcv, ty_snd, ty_rcv,
    p_snd, p_rcv, s_snd, s_rcv, g_snd, g_rcv, f_snd, f_rcv,
):
    y, z = lax.axis_index("groups"), lax.axis_index("vocab")
    x, c = lax.axis_index("dp"), lax.axis_index("rep")
    p = 2 * x + c
    cols = tab.shape[1]
    block = tab.shape[0]
    half = block // 2
    near = {1: (x, 1 - c), 2: (1 - x, c), 3: (1 - x, 1 - c)}
    near_id = {k: {"dp": a, "rep": b} for k, (a, b) in near.items()}
    place = {0: p, **{k: 2 * a + b for k, (a, b) in near.items()}}
    up_id = {d: {"vocab": lax.rem(z + d, 4)} for d in (1, 2, 3)}
    down = {d: lax.rem(z + 4 - d, 4) for d in (1, 2, 3)}
    twin = {"groups": 1 - y}

    def remote(src, dst, snd, rcv, to):
        return pltpu.make_async_remote_copy(
            src_ref=src, dst_ref=dst, send_sem=snd, recv_sem=rcv, device_id=to, device_id_type=MESH
        )

    def my_cols(q):
        return pl.ds(pl.multiple_of(q * cols, 128), cols)

    own = [
        pltpu.make_async_copy(hid.at[:, my_cols(p)], hcols.at[p], loc_sem.at[0]),
        pltpu.make_async_copy(tab, tall.at[z], loc_sem.at[1]),
        pltpu.make_async_copy(cot.at[:, my_cols(p)], gcols.at[p], loc_sem.at[2]),
    ]
    for copy in own:
        copy.start()

    barrier = pltpu.get_barrier_semaphore()
    for to in (*near_id.values(), *up_id.values(), twin):
        pl.semaphore_signal(barrier, inc=1, device_id=to, device_id_type=MESH)
    pl.semaphore_wait(barrier, 7)

    send_h = {
        k: remote(hid.at[:, my_cols(place[k])], hcols.at[p], h_snd.at[k], h_rcv.at[k], near_id[k])
        for k in (2, 3, 1)
    }
    for copy in send_h.values():
        copy.start()

    def strip(part):
        return pl.ds(pl.multiple_of(half * y + half // 2 * part, half // 2), half // 2)

    def relay(s, way, part):
        row = z - way * (s - 1)
        src = tab.at[strip(part)] if s == 1 else tall.at[row, strip(part)]
        lane = (s if way == 1 else s + 4) + 8 * part
        copy = remote(src, tall.at[row, strip(part)], tz_snd.at[lane], tz_rcv.at[lane], {"vocab": z + way})
        on = (z < 3) & (row >= 0) if way == 1 else (z > 0) & (row <= 3)
        return on, copy

    def landed(s, way, part):
        row = z - way * s
        piece = tall.at[row, strip(part)]
        lane = (s if way == 1 else s + 4) + 8 * part
        came = remote(piece, piece, tz_snd.at[lane], tz_rcv.at[lane], {"vocab": z + way})
        over = remote(piece, piece, ty_snd.at[lane], ty_rcv.at[lane], twin)
        on = row >= 0 if way == 1 else row <= 3
        return on, came, over

    def pass_on(s, part):
        for way in (1, -1):
            on, came, over = landed(s, way, part)

            @pl.when(on)
            def _():
                came.wait_recv()
                over.start()

            if s < 3:
                on, copy = relay(s + 1, way, part)

                @pl.when(on)
                def _():
                    copy.start()

    for part_of in (0, 1):
        for way in (1, -1):
            on, copy = relay(1, way, part_of)

            @pl.when(on)
            def _():
                copy.start()

    ids = jnp.broadcast_to(tgt[...].astype(jnp.float32), (128, tgt.shape[1]))
    tcol[...] = ids.T

    for copy in own:
        copy.wait()
    send_p = {}
    for k in (0, 1, 2, 3):
        if k == 2:
            pass_on(1, 0)
        if k:
            send_h[k].wait_recv()
        part[k] = lax.dot_general(
            hcols[place[k]], tall[z], (((1,), (1,)), ((), ())), preferred_element_type=jnp.float32
        )
        if k:
            send_p[k] = remote(part.at[k], rawin.at[k], p_snd.at[k], p_rcv.at[k], near_id[k])
            send_p[k].start()
    send_c = {
        k: remote(cot.at[:, my_cols(place[k])], gcols.at[p], c_snd.at[k], c_rcv.at[k], near_id[k])
        for k in (2, 3, 1)
    }
    for copy in send_c.values():
        copy.start()
    pass_on(1, 1)

    raw = part[0]
    for k in (1, 2, 3):
        send_p[k].wait_recv()
        raw = raw + rawin[k]
    squash = jnp.tanh(raw / CAP)
    expo = jnp.exp(CAP * squash)
    line = jnp.broadcast_to(jnp.sum(expo, axis=1, keepdims=True), (ROW_LEN, 128))
    tot[0] = jnp.concatenate([line, line], axis=0).T[:8]
    send_s = {d: remote(tot.at[0], tot.at[d], s_snd.at[d], s_rcv.at[d], up_id[d]) for d in (1, 2, 3)}
    for copy in send_s.values():
        copy.start()
    target = tcol[pl.ds(pl.multiple_of(ROW_LEN * p, ROW_LEN), ROW_LEN), :]
    target = jnp.concatenate([target] * (block // 128), axis=1)
    row_ids = (z * block + lax.broadcasted_iota(jnp.int32, (ROW_LEN, block), 1)).astype(jnp.float32)
    hit = (target == row_ids).astype(jnp.float32)
    count = jnp.full((ROW_LEN, block), cnt[p], jnp.int32)
    slot = lax.broadcasted_iota(jnp.int32, (ROW_LEN, block), 0)
    weight = jnp.where(slot < count, ROW_LEN / count.astype(jnp.float32), 0.0)
    slope = 1.0 - squash * squash
    for copy in send_s.values():
        copy.wait_recv()
    whole = tot[0] + tot[1] + tot[2] + tot[3]
    whole = jnp.broadcast_to(whole[:1], (128, 128)).T[:ROW_LEN]
    whole = jnp.concatenate([whole] * (block // 128), axis=1)
    gall[z, p] = (weight * (expo / whole - hit) * slope).astype(jnp.bfloat16)

    send_g = {d: remote(gall.at[z, p], gall.at[z, p], g_snd.at[d], g_rcv.at[d], up_id[d]) for d in (1, 2, 3)}
    for copy in send_g.values():
        copy.start()
    send_f = {}

    def hand_on(d, row, k):
        piece = gall.at[row, place[2] if k == 3 else p]
        to = near_id[1 if k == 3 else k]
        send_f[d, k] = remote(piece, piece, f_snd.at[d, k], f_rcv.at[d, k], to)
        send_f[d, k].start()

    hand_on(0, z, 2)
    hand_on(0, z, 1)
    pass_on(2, 0)
    for d in (1, 3, 2):
        send_g[d].wait_recv()
        hand_on(d, down[d], 2)
        hand_on(d, down[d], 1)
    pass_on(2, 1)
    for d in (0, 1, 3, 2):
        send_f[d, 2].wait_recv()
        hand_on(d, down[d] if d else z, 3)
    pass_on(3, 0)
    pass_on(3, 1)

    for k in (2, 3, 1):
        send_c[k].wait_recv()
    for k in (1, 3):
        send_f[0, k].wait_recv()
    tokens = tok.shape[1]
    vocab_ids = z * block + lax.broadcasted_iota(jnp.int32, (block, tokens), 0)
    one_hot = (jnp.broadcast_to(tok[...], (block, tokens)) == vocab_ids).astype(jnp.float32)
    one_hot = one_hot.astype(jnp.bfloat16)
    grads = gall[z].reshape(tokens, block)

    @pl.loop(0, cols // TILE)
    def _(j):
        at = pl.ds(pl.multiple_of(j * TILE, 128), TILE)
        head = lax.dot_general(
            grads, hcols[:, :, at].reshape(tokens, TILE), (((0,), (0,)), ((), ())),
            preferred_element_type=jnp.float32,
        )
        embed = jnp.dot(
            one_hot, gcols[:, :, at].reshape(tokens, TILE), preferred_element_type=jnp.float32
        )
        tab_out[:, at] = (head + math.sqrt(D) * embed).astype(jnp.bfloat16)

    for d in (1, 3, 2):
        for k in (1, 3):
            send_f[d, k].wait_recv()
    for s, part_of in [(s, part_of) for s in (1, 2, 3) for part_of in (0, 1)]:
        for way in (1, -1):
            on, _, over = landed(s, way, part_of)

            @pl.when(on)
            def _():
                over.wait()

            on, copy = relay(s, way, part_of)

            @pl.when(on)
            def _():
                copy.wait_send()

    @pl.loop(0, cols // TILE)
    def _(j):
        at = pl.ds(pl.multiple_of(j * TILE, 128), TILE)
        total = jnp.zeros((tokens, TILE), jnp.float32)
        for row in range(4):
            total = total + jnp.dot(
                gall[row].reshape(tokens, block), tall[row, :, at], preferred_element_type=jnp.float32
            )
        hid_out[:, at] = total.astype(jnp.bfloat16)

    for group in (send_h, send_p, send_c, send_s, send_g, send_f):
        for copy in group.values():
            copy.wait_send()


def shards(hidden, cotangent, table, token_ids, target_ids, row_counts):
    block, cols = table.shape
    rows = hidden.shape[0]
    tokens = token_ids.shape[0]
    vmem = pl.BlockSpec(memory_space=pltpu.VMEM)
    hbm = pl.BlockSpec(memory_space=pl.ANY)
    dma = pltpu.SemaphoreType.DMA
    return pl.pallas_call(
        kernel,
        out_shape=(
            jax.ShapeDtypeStruct((tokens, cols), jnp.bfloat16),
            jax.ShapeDtypeStruct((block, cols), jnp.bfloat16),
        ),
        in_specs=[hbm, hbm, hbm, vmem, vmem, pl.BlockSpec(memory_space=pltpu.SMEM)],
        out_specs=(vmem, vmem),
        scratch_shapes=[
            pltpu.VMEM((4, block, cols), jnp.bfloat16),
            pltpu.VMEM((4, rows, cols), jnp.bfloat16),
            pltpu.VMEM((4, rows, cols), jnp.bfloat16),
            pltpu.VMEM((4, rows, block), jnp.float32),
            pltpu.VMEM((4, rows, block), jnp.float32),
            pltpu.VMEM((4, 8, 128), jnp.float32),
            pltpu.VMEM((4, 4, rows, block), jnp.bfloat16),
            pltpu.VMEM((tokens, 128), jnp.float32),
            dma((3,)),
            *[dma((4,))] * 4,
            *[dma((16,))] * 4,
            *[dma((4,))] * 6,
            dma((4, 4)),
            dma((4, 4)),
        ],
        compiler_params=pltpu.CompilerParams(
            collective_id=0, has_side_effects=True, vmem_limit_bytes=60 * 1024 * 1024
        ),
        cost_estimate=pl.CostEstimate(flops=1200000000, bytes_accessed=6000000, transcendentals=40000),
    )(hidden, cotangent, table, token_ids[None, :], target_ids[None, :], row_counts)


def solution(mesh):
    sizes = tuple(mesh.shape[axis] for axis in ("groups", "vocab", "dp", "rep"))

    def part(hidden, cotangent, table, token_ids, target_ids, row_counts):
        block, cols = table.shape
        fits = (
            sizes == (2, 4, 2, 2)
            and hidden.shape[0] == ROW_LEN
            and cols % TILE == 0
            and block == 256
            and token_ids.shape[0] == 256
        )
        run = shards if fits else plain
        return run(hidden, cotangent, table, token_ids, target_ids, row_counts)

    in_specs = (
        P(("groups", "dp", "rep"), None),
        P(("groups", "dp", "rep"), None),
        P("vocab", ("dp", "rep")),
        P("groups"),
        P("groups"),
        P("groups"),
    )
    out_specs = (P("groups", ("dp", "rep")), P(("groups", "vocab"), ("dp", "rep")))
    return jax.shard_map(part, mesh=mesh, in_specs=in_specs, out_specs=out_specs, check_vma=False)
```

```python
import math

import jax
import jax.numpy as jnp
from jax import lax
from jax.experimental import pallas as pl
from jax.experimental.pallas import tpu as pltpu
from jax.sharding import PartitionSpec as P

D = 4608
CAP = 30
ROW_LEN = 64


def token_weights(row_counts):
    slots = jnp.arange(ROW_LEN, dtype=jnp.int32)[None, :]
    counts = row_counts[:, None]
    scale = ROW_LEN / counts.astype(jnp.float32)
    return jnp.where(slots < counts, scale, jnp.float32(0.0)).reshape(-1)


def plain(hidden, cotangent, table, token_ids, target_ids, row_counts):
    h_cols, g_cols = (
        lax.all_to_all(hidden, ("dp", "rep"), split_axis=1, concat_axis=0, tiled=True),
        lax.all_to_all(cotangent, ("dp", "rep"), split_axis=1, concat_axis=0, tiled=True),
    )
    block = table.shape[0]
    parts = lax.axis_size(("dp", "rep"))
    base = lax.axis_index("vocab") * block
    weight = token_weights(row_counts)
    span = block // parts
    raw = lax.psum_scatter(
        lax.dot_general(
            table, h_cols, (((1,), (1,)), ((), ())), preferred_element_type=jnp.float32
        ),
        ("dp", "rep"),
        scatter_dimension=0,
        tiled=True,
    )
    first = base + lax.axis_index(("dp", "rep")) * span
    squash = jnp.tanh(raw / CAP)
    expo = jnp.exp(CAP * squash)
    total = lax.psum(jnp.sum(expo, axis=0), ("vocab", "dp", "rep"))
    row_ids = first + jnp.arange(span, dtype=jnp.int32)
    hit = (target_ids[None, :] == row_ids[:, None]).astype(jnp.float32)
    grad = (weight[None, :] * (expo / total[None, :] - hit) * (1.0 - squash * squash)).astype(
        jnp.bfloat16
    )
    grads = lax.all_gather(grad, ("dp", "rep"), axis=0, tiled=True)
    head = jnp.dot(grads, h_cols, preferred_element_type=jnp.float32)
    partial_sum = lax.dot_general(
        grads, table, (((0,), (0,)), ((), ())), preferred_element_type=jnp.float32
    )
    block_ids = base + jnp.arange(block, dtype=jnp.int32)
    one_hot = (token_ids[:, None] == block_ids[None, :]).astype(jnp.bfloat16)
    embed = lax.dot_general(
        one_hot, g_cols, (((0,), (0,)), ((), ())), preferred_element_type=jnp.float32
    )
    table_grad = (head + math.sqrt(D) * embed).astype(jnp.bfloat16)
    hidden_grad = lax.psum(partial_sum, "vocab").astype(jnp.bfloat16)
    return (hidden_grad, table_grad)


MESH = pl.DeviceIdType.MESH
TILE = 384


def kernel(
    hid, cot, tab, tok, tgt, cnt,
    hid_out, tab_out,
    tall, hcols, gcols, part, rawin, tot, gall, tcol,
    loc_sem, h_snd, h_rcv, c_snd, c_rcv, tz_snd, tz_rcv, ty_snd, ty_rcv,
    p_snd, p_rcv, s_snd, s_rcv, g_snd, g_rcv, f_snd, f_rcv,
):
    y, z = lax.axis_index("groups"), lax.axis_index("vocab")
    x, c = lax.axis_index("dp"), lax.axis_index("rep")
    p = 2 * x + c
    cols = tab.shape[1]
    block = tab.shape[0]
    half = block // 2
    near = {1: (x, 1 - c), 2: (1 - x, c), 3: (1 - x, 1 - c)}
    near_id = {k: {"dp": a, "rep": b} for k, (a, b) in near.items()}
    place = {0: p, **{k: 2 * a + b for k, (a, b) in near.items()}}
    up_id = {d: {"vocab": lax.rem(z + d, 4)} for d in (1, 2, 3)}
    down = {d: lax.rem(z + 4 - d, 4) for d in (1, 2, 3)}
    twin = {"groups": 1 - y}

    def remote(src, dst, snd, rcv, to):
        return pltpu.make_async_remote_copy(
            src_ref=src, dst_ref=dst, send_sem=snd, recv_sem=rcv, device_id=to, device_id_type=MESH
        )

    def my_cols(q):
        return pl.ds(pl.multiple_of(q * cols, 128), cols)

    own = [
        pltpu.make_async_copy(hid.at[:, my_cols(p)], hcols.at[p], loc_sem.at[0]),
        pltpu.make_async_copy(tab, tall.at[z], loc_sem.at[1]),
        pltpu.make_async_copy(cot.at[:, my_cols(p)], gcols.at[p], loc_sem.at[2]),
    ]
    for copy in own:
        copy.start()

    barrier = pltpu.get_barrier_semaphore()
    for to in (*near_id.values(), *up_id.values(), twin):
        pl.semaphore_signal(barrier, inc=1, device_id=to, device_id_type=MESH)
    pl.semaphore_wait(barrier, 7)

    send_h = {
        k: remote(hid.at[:, my_cols(place[k])], hcols.at[p], h_snd.at[k], h_rcv.at[k], near_id[k])
        for k in (2, 3, 1)
    }
    for copy in send_h.values():
        copy.start()

    def strip(part):
        return pl.ds(pl.multiple_of(half * y + half // 2 * part, half // 2), half // 2)

    def relay(s, way, part):
        row = z - way * (s - 1)
        src = tab.at[strip(part)] if s == 1 else tall.at[row, strip(part)]
        lane = (s if way == 1 else s + 4) + 8 * part
        copy = remote(src, tall.at[row, strip(part)], tz_snd.at[lane], tz_rcv.at[lane], {"vocab": z + way})
        on = (z < 3) & (row >= 0) if way == 1 else (z > 0) & (row <= 3)
        return on, copy

    def landed(s, way, part):
        row = z - way * s
        piece = tall.at[row, strip(part)]
        lane = (s if way == 1 else s + 4) + 8 * part
        came = remote(piece, piece, tz_snd.at[lane], tz_rcv.at[lane], {"vocab": z + way})
        over = remote(piece, piece, ty_snd.at[lane], ty_rcv.at[lane], twin)
        on = row >= 0 if way == 1 else row <= 3
        return on, came, over

    def pass_on(s, part):
        for way in (1, -1):
            on, came, over = landed(s, way, part)

            @pl.when(on)
            def _():
                came.wait_recv()
                over.start()

            if s < 3:
                on, copy = relay(s + 1, way, part)

                @pl.when(on)
                def _():
                    copy.start()

    for part_of in (0, 1):
        for way in (1, -1):
            on, copy = relay(1, way, part_of)

            @pl.when(on)
            def _():
                copy.start()

    ids = jnp.broadcast_to(tgt[...].astype(jnp.float32), (128, tgt.shape[1]))
    tcol[...] = ids.T

    for copy in own:
        copy.wait()
    send_p = {}
    for k in (0, 1, 2, 3):
        if k == 2:
            pass_on(1, 0)
        if k:
            send_h[k].wait_recv()
        part[k] = lax.dot_general(
            hcols[place[k]], tall[z], (((1,), (1,)), ((), ())), preferred_element_type=jnp.float32
        )
        if k:
            send_p[k] = remote(part.at[k], rawin.at[k], p_snd.at[k], p_rcv.at[k], near_id[k])
            send_p[k].start()
    send_c = {
        k: remote(cot.at[:, my_cols(place[k])], gcols.at[p], c_snd.at[k], c_rcv.at[k], near_id[k])
        for k in (2, 3, 1)
    }
    for copy in send_c.values():
        copy.start()
    pass_on(1, 1)

    raw = part[0]
    for k in (1, 2, 3):
        send_p[k].wait_recv()
        raw = raw + rawin[k]
    squash = jnp.tanh(raw / CAP)
    expo = jnp.exp(CAP * squash)
    line = jnp.broadcast_to(jnp.sum(expo, axis=1, keepdims=True), (ROW_LEN, 128))
    tot[0] = jnp.concatenate([line, line], axis=0).T[:8]
    send_s = {d: remote(tot.at[0], tot.at[d], s_snd.at[d], s_rcv.at[d], up_id[d]) for d in (1, 2, 3)}
    for copy in send_s.values():
        copy.start()
    target = tcol[pl.ds(pl.multiple_of(ROW_LEN * p, ROW_LEN), ROW_LEN), :]
    target = jnp.concatenate([target] * (block // 128), axis=1)
    row_ids = (z * block + lax.broadcasted_iota(jnp.int32, (ROW_LEN, block), 1)).astype(jnp.float32)
    hit = (target == row_ids).astype(jnp.float32)
    count = jnp.full((ROW_LEN, block), cnt[p], jnp.int32)
    slot = lax.broadcasted_iota(jnp.int32, (ROW_LEN, block), 0)
    weight = jnp.where(slot < count, ROW_LEN / count.astype(jnp.float32), 0.0)
    slope = 1.0 - squash * squash
    for copy in send_s.values():
        copy.wait_recv()
    whole = tot[0] + tot[1] + tot[2] + tot[3]
    whole = jnp.broadcast_to(whole[:1], (128, 128)).T[:ROW_LEN]
    whole = jnp.concatenate([whole] * (block // 128), axis=1)
    gall[z, p] = (weight * (expo / whole - hit) * slope).astype(jnp.bfloat16)

    send_g = {d: remote(gall.at[z, p], gall.at[z, p], g_snd.at[d], g_rcv.at[d], up_id[d]) for d in (1, 2, 3)}
    for copy in send_g.values():
        copy.start()
    send_f = {}

    def hand_on(d, row, k):
        piece = gall.at[row, place[2] if k == 3 else p]
        to = near_id[1 if k == 3 else k]
        send_f[d, k] = remote(piece, piece, f_snd.at[d, k], f_rcv.at[d, k], to)
        send_f[d, k].start()

    hand_on(0, z, 2)
    hand_on(0, z, 1)
    pass_on(2, 0)
    for d in (1, 3, 2):
        send_g[d].wait_recv()
        hand_on(d, down[d], 2)
        hand_on(d, down[d], 1)
    pass_on(2, 1)
    for d in (0, 1, 3, 2):
        send_f[d, 2].wait_recv()
        hand_on(d, down[d] if d else z, 3)
        if d == 1:
            pass_on(3, 0)
    pass_on(3, 1)

    for k in (2, 3, 1):
        send_c[k].wait_recv()
    for k in (1, 3):
        send_f[0, k].wait_recv()
    tokens = tok.shape[1]
    vocab_ids = z * block + lax.broadcasted_iota(jnp.int32, (block, tokens), 0)
    one_hot = (jnp.broadcast_to(tok[...], (block, tokens)) == vocab_ids).astype(jnp.float32)
    one_hot = one_hot.astype(jnp.bfloat16)
    grads = gall[z].reshape(tokens, block)

    @pl.loop(0, cols // TILE)
    def _(j):
        at = pl.ds(pl.multiple_of(j * TILE, 128), TILE)
        head = lax.dot_general(
            grads, hcols[:, :, at].reshape(tokens, TILE), (((0,), (0,)), ((), ())),
            preferred_element_type=jnp.float32,
        )
        embed = jnp.dot(
            one_hot, gcols[:, :, at].reshape(tokens, TILE), preferred_element_type=jnp.float32
        )
        tab_out[:, at] = (head + math.sqrt(D) * embed).astype(jnp.bfloat16)

    for d in (1, 3, 2):
        for k in (1, 3):
            send_f[d, k].wait_recv()
    for s, part_of in [(s, part_of) for s in (1, 2, 3) for part_of in (0, 1)]:
        for way in (1, -1):
            on, _, over = landed(s, way, part_of)

            @pl.when(on)
            def _():
                over.wait()

            on, copy = relay(s, way, part_of)

            @pl.when(on)
            def _():
                copy.wait_send()

    @pl.loop(0, cols // TILE)
    def _(j):
        at = pl.ds(pl.multiple_of(j * TILE, 128), TILE)
        total = jnp.zeros((tokens, TILE), jnp.float32)
        for row in range(4):
            total = total + jnp.dot(
                gall[row].reshape(tokens, block), tall[row, :, at], preferred_element_type=jnp.float32
            )
        hid_out[:, at] = total.astype(jnp.bfloat16)

    for group in (send_h, send_p, send_c, send_s, send_g, send_f):
        for copy in group.values():
            copy.wait_send()


def hand_out(hid, tab, hid_out, tab_out):
    hid_out[...] = hid[...]
    tab_out[...] = tab[...]


def shards(hidden, cotangent, table, token_ids, target_ids, row_counts):
    block, cols = table.shape
    rows = hidden.shape[0]
    tokens = token_ids.shape[0]
    vmem = pl.BlockSpec(memory_space=pltpu.VMEM)
    hbm = pl.BlockSpec(memory_space=pl.ANY)
    dma = pltpu.SemaphoreType.DMA
    results = pl.pallas_call(
        kernel,
        out_shape=(
            jax.ShapeDtypeStruct((tokens, cols), jnp.bfloat16),
            jax.ShapeDtypeStruct((block, cols), jnp.bfloat16),
        ),
        in_specs=[hbm, hbm, hbm, vmem, vmem, pl.BlockSpec(memory_space=pltpu.SMEM)],
        out_specs=(vmem, vmem),
        scratch_shapes=[
            pltpu.VMEM((4, block, cols), jnp.bfloat16),
            pltpu.VMEM((4, rows, cols), jnp.bfloat16),
            pltpu.VMEM((4, rows, cols), jnp.bfloat16),
            pltpu.VMEM((4, rows, block), jnp.float32),
            pltpu.VMEM((4, rows, block), jnp.float32),
            pltpu.VMEM((4, 8, 128), jnp.float32),
            pltpu.VMEM((4, 4, rows, block), jnp.bfloat16),
            pltpu.VMEM((tokens, 128), jnp.float32),
            dma((3,)),
            *[dma((4,))] * 4,
            *[dma((16,))] * 4,
            *[dma((4,))] * 6,
            dma((4, 4)),
            dma((4, 4)),
        ],
        compiler_params=pltpu.CompilerParams(
            collective_id=0, has_side_effects=True, vmem_limit_bytes=60 * 1024 * 1024
        ),
        cost_estimate=pl.CostEstimate(flops=1200000000, bytes_accessed=6000000, transcendentals=40000),
    )(hidden, cotangent, table, token_ids[None, :], target_ids[None, :], row_counts)
    return pl.pallas_call(
        hand_out,
        out_shape=tuple(jax.ShapeDtypeStruct(a.shape, a.dtype) for a in results),
        grid=(2,),
        in_specs=[pl.BlockSpec((a.shape[0] // 2, cols), lambda i: (i, 0)) for a in results],
        out_specs=tuple(pl.BlockSpec((a.shape[0] // 2, cols), lambda i: (i, 0)) for a in results),
    )(*results)


def solution(mesh):
    sizes = tuple(mesh.shape[axis] for axis in ("groups", "vocab", "dp", "rep"))

    def part(hidden, cotangent, table, token_ids, target_ids, row_counts):
        block, cols = table.shape
        fits = (
            sizes == (2, 4, 2, 2)
            and hidden.shape[0] == ROW_LEN
            and cols % TILE == 0
            and block == 256
            and token_ids.shape[0] == 256
        )
        run = shards if fits else plain
        return run(hidden, cotangent, table, token_ids, target_ids, row_counts)

    in_specs = (
        P(("groups", "dp", "rep"), None),
        P(("groups", "dp", "rep"), None),
        P("vocab", ("dp", "rep")),
        P("groups"),
        P("groups"),
        P("groups"),
    )
    out_specs = (P("groups", ("dp", "rep")), P(("groups", "vocab"), ("dp", "rep")))
    return jax.shard_map(part, mesh=mesh, in_specs=in_specs, out_specs=out_specs, check_vma=False)
```

```python
import math

import jax
import jax.numpy as jnp
from jax import lax
from jax.experimental import pallas as pl
from jax.experimental.pallas import tpu as pltpu
from jax.sharding import PartitionSpec as P

D = 4608
CAP = 30
ROW_LEN = 64


def token_weights(row_counts):
    slots = jnp.arange(ROW_LEN, dtype=jnp.int32)[None, :]
    counts = row_counts[:, None]
    scale = ROW_LEN / counts.astype(jnp.float32)
    return jnp.where(slots < counts, scale, jnp.float32(0.0)).reshape(-1)


def plain(hidden, cotangent, table, token_ids, target_ids, row_counts):
    h_cols, g_cols = (
        lax.all_to_all(hidden, ("dp", "rep"), split_axis=1, concat_axis=0, tiled=True),
        lax.all_to_all(cotangent, ("dp", "rep"), split_axis=1, concat_axis=0, tiled=True),
    )
    block = table.shape[0]
    parts = lax.axis_size(("dp", "rep"))
    base = lax.axis_index("vocab") * block
    weight = token_weights(row_counts)
    span = block // parts
    raw = lax.psum_scatter(
        lax.dot_general(
            table, h_cols, (((1,), (1,)), ((), ())), preferred_element_type=jnp.float32
        ),
        ("dp", "rep"),
        scatter_dimension=0,
        tiled=True,
    )
    first = base + lax.axis_index(("dp", "rep")) * span
    squash = jnp.tanh(raw / CAP)
    expo = jnp.exp(CAP * squash)
    total = lax.psum(jnp.sum(expo, axis=0), ("vocab", "dp", "rep"))
    row_ids = first + jnp.arange(span, dtype=jnp.int32)
    hit = (target_ids[None, :] == row_ids[:, None]).astype(jnp.float32)
    grad = (weight[None, :] * (expo / total[None, :] - hit) * (1.0 - squash * squash)).astype(
        jnp.bfloat16
    )
    grads = lax.all_gather(grad, ("dp", "rep"), axis=0, tiled=True)
    head = jnp.dot(grads, h_cols, preferred_element_type=jnp.float32)
    partial_sum = lax.dot_general(
        grads, table, (((0,), (0,)), ((), ())), preferred_element_type=jnp.float32
    )
    block_ids = base + jnp.arange(block, dtype=jnp.int32)
    one_hot = (token_ids[:, None] == block_ids[None, :]).astype(jnp.bfloat16)
    embed = lax.dot_general(
        one_hot, g_cols, (((0,), (0,)), ((), ())), preferred_element_type=jnp.float32
    )
    table_grad = (head + math.sqrt(D) * embed).astype(jnp.bfloat16)
    hidden_grad = lax.psum(partial_sum, "vocab").astype(jnp.bfloat16)
    return (hidden_grad, table_grad)


MESH = pl.DeviceIdType.MESH
TILE = 384


def kernel(
    hid, cot, tab, tok, tgt, cnt,
    hid_out, tab_out,
    tall, hcols, gcols, part, rawin, tot, gall, tcol,
    loc_sem, h_snd, h_rcv, c_snd, c_rcv, tz_snd, tz_rcv, ty_snd, ty_rcv,
    p_snd, p_rcv, s_snd, s_rcv, g_snd, g_rcv, f_snd, f_rcv,
):
    y, z = lax.axis_index("groups"), lax.axis_index("vocab")
    x, c = lax.axis_index("dp"), lax.axis_index("rep")
    p = 2 * x + c
    cols = tab.shape[1]
    block = tab.shape[0]
    half = block // 2
    near = {1: (x, 1 - c), 2: (1 - x, c), 3: (1 - x, 1 - c)}
    near_id = {k: {"dp": a, "rep": b} for k, (a, b) in near.items()}
    place = {0: p, **{k: 2 * a + b for k, (a, b) in near.items()}}
    up_id = {d: {"vocab": lax.rem(z + d, 4)} for d in (1, 2, 3)}
    down = {d: lax.rem(z + 4 - d, 4) for d in (1, 2, 3)}
    twin = {"groups": 1 - y}

    def remote(src, dst, snd, rcv, to):
        return pltpu.make_async_remote_copy(
            src_ref=src, dst_ref=dst, send_sem=snd, recv_sem=rcv, device_id=to, device_id_type=MESH
        )

    def my_cols(q):
        return pl.ds(pl.multiple_of(q * cols, 128), cols)

    own = [
        pltpu.make_async_copy(hid.at[:, my_cols(p)], hcols.at[p], loc_sem.at[0]),
        pltpu.make_async_copy(tab, tall.at[z], loc_sem.at[1]),
        pltpu.make_async_copy(cot.at[:, my_cols(p)], gcols.at[p], loc_sem.at[2]),
    ]
    for copy in own:
        copy.start()

    barrier = pltpu.get_barrier_semaphore()
    for to in (*near_id.values(), *up_id.values(), twin):
        pl.semaphore_signal(barrier, inc=1, device_id=to, device_id_type=MESH)
    pl.semaphore_wait(barrier, 7)

    send_h = {
        k: remote(hid.at[:, my_cols(place[k])], hcols.at[p], h_snd.at[k], h_rcv.at[k], near_id[k])
        for k in (2, 3, 1)
    }
    for copy in send_h.values():
        copy.start()

    def strip(part):
        return pl.ds(pl.multiple_of(half * y + half // 2 * part, half // 2), half // 2)

    def relay(s, way, part):
        row = z - way * (s - 1)
        src = tab.at[strip(part)] if s == 1 else tall.at[row, strip(part)]
        lane = (s if way == 1 else s + 4) + 8 * part
        copy = remote(src, tall.at[row, strip(part)], tz_snd.at[lane], tz_rcv.at[lane], {"vocab": z + way})
        on = (z < 3) & (row >= 0) if way == 1 else (z > 0) & (row <= 3)
        return on, copy

    def landed(s, way, part):
        row = z - way * s
        piece = tall.at[row, strip(part)]
        lane = (s if way == 1 else s + 4) + 8 * part
        came = remote(piece, piece, tz_snd.at[lane], tz_rcv.at[lane], {"vocab": z + way})
        over = remote(piece, piece, ty_snd.at[lane], ty_rcv.at[lane], twin)
        on = row >= 0 if way == 1 else row <= 3
        return on, came, over

    def pass_on(s, part):
        for way in (1, -1):
            on, came, over = landed(s, way, part)

            @pl.when(on)
            def _():
                came.wait_recv()
                over.start()

            if s < 3:
                on, copy = relay(s + 1, way, part)

                @pl.when(on)
                def _():
                    copy.start()

    for part_of in (0, 1):
        for way in (1, -1):
            on, copy = relay(1, way, part_of)

            @pl.when(on)
            def _():
                copy.start()

    ids = jnp.broadcast_to(tgt[...].astype(jnp.float32), (128, tgt.shape[1]))
    tcol[...] = ids.T

    for copy in own:
        copy.wait()
    send_p = {}
    for k in (0, 1, 2, 3):
        if k == 2:
            pass_on(1, 0)
        if k:
            send_h[k].wait_recv()
        part[k] = lax.dot_general(
            hcols[place[k]], tall[z], (((1,), (1,)), ((), ())), preferred_element_type=jnp.float32
        )
        if k:
            send_p[k] = remote(part.at[k], rawin.at[k], p_snd.at[k], p_rcv.at[k], near_id[k])
            send_p[k].start()
    send_c = {
        k: remote(cot.at[:, my_cols(place[k])], gcols.at[p], c_snd.at[k], c_rcv.at[k], near_id[k])
        for k in (2, 3, 1)
    }
    for copy in send_c.values():
        copy.start()
    pass_on(1, 1)

    raw = part[0]
    for k in (1, 2, 3):
        send_p[k].wait_recv()
        raw = raw + rawin[k]
    squash = jnp.tanh(raw / CAP)
    expo = jnp.exp(CAP * squash)
    line = jnp.broadcast_to(jnp.sum(expo, axis=1, keepdims=True), (ROW_LEN, 128))
    tot[0] = jnp.concatenate([line, line], axis=0).T[:8]
    send_s = {d: remote(tot.at[0], tot.at[d], s_snd.at[d], s_rcv.at[d], up_id[d]) for d in (1, 2, 3)}
    for copy in send_s.values():
        copy.start()
    target = tcol[pl.ds(pl.multiple_of(ROW_LEN * p, ROW_LEN), ROW_LEN), :]
    target = jnp.concatenate([target] * (block // 128), axis=1)
    row_ids = (z * block + lax.broadcasted_iota(jnp.int32, (ROW_LEN, block), 1)).astype(jnp.float32)
    hit = (target == row_ids).astype(jnp.float32)
    count = jnp.full((ROW_LEN, block), cnt[p], jnp.int32)
    slot = lax.broadcasted_iota(jnp.int32, (ROW_LEN, block), 0)
    weight = jnp.where(slot < count, ROW_LEN / count.astype(jnp.float32), 0.0)
    slope = 1.0 - squash * squash
    pass_on(2, 0)
    for copy in send_s.values():
        copy.wait_recv()
    whole = tot[0] + tot[1] + tot[2] + tot[3]
    whole = jnp.broadcast_to(whole[:1], (128, 128)).T[:ROW_LEN]
    whole = jnp.concatenate([whole] * (block // 128), axis=1)
    gall[z, p] = (weight * (expo / whole - hit) * slope).astype(jnp.bfloat16)

    send_g = {d: remote(gall.at[z, p], gall.at[z, p], g_snd.at[d], g_rcv.at[d], up_id[d]) for d in (1, 2, 3)}
    for copy in send_g.values():
        copy.start()
    send_f = {}

    def hand_on(d, row, k):
        piece = gall.at[row, place[2] if k == 3 else p]
        to = near_id[1 if k == 3 else k]
        send_f[d, k] = remote(piece, piece, f_snd.at[d, k], f_rcv.at[d, k], to)
        send_f[d, k].start()

    hand_on(0, z, 2)
    hand_on(0, z, 1)
    for d in (1, 3, 2):
        send_g[d].wait_recv()
        hand_on(d, down[d], 2)
        hand_on(d, down[d], 1)
    pass_on(2, 1)
    for d in (0, 1, 3, 2):
        send_f[d, 2].wait_recv()
        hand_on(d, down[d] if d else z, 3)
        if d == 1:
            pass_on(3, 0)
    pass_on(3, 1)

    for k in (2, 3, 1):
        send_c[k].wait_recv()
    for k in (1, 3):
        send_f[0, k].wait_recv()
    tokens = tok.shape[1]
    vocab_ids = z * block + lax.broadcasted_iota(jnp.int32, (block, tokens), 0)
    one_hot = (jnp.broadcast_to(tok[...], (block, tokens)) == vocab_ids).astype(jnp.float32)
    one_hot = one_hot.astype(jnp.bfloat16)
    grads = gall[z].reshape(tokens, block)

    @pl.loop(0, cols // TILE)
    def _(j):
        at = pl.ds(pl.multiple_of(j * TILE, 128), TILE)
        head = lax.dot_general(
            grads, hcols[:, :, at].reshape(tokens, TILE), (((0,), (0,)), ((), ())),
            preferred_element_type=jnp.float32,
        )
        embed = jnp.dot(
            one_hot, gcols[:, :, at].reshape(tokens, TILE), preferred_element_type=jnp.float32
        )
        tab_out[:, at] = (head + math.sqrt(D) * embed).astype(jnp.bfloat16)

    for d in (1, 3, 2):
        for k in (1, 3):
            send_f[d, k].wait_recv()
    for s, part_of in [(s, part_of) for s in (1, 2, 3) for part_of in (0, 1)]:
        for way in (1, -1):
            on, _, over = landed(s, way, part_of)

            @pl.when(on)
            def _():
                over.wait()

            on, copy = relay(s, way, part_of)

            @pl.when(on)
            def _():
                copy.wait_send()

    @pl.loop(0, cols // TILE)
    def _(j):
        at = pl.ds(pl.multiple_of(j * TILE, 128), TILE)
        total = jnp.zeros((tokens, TILE), jnp.float32)
        for row in range(4):
            total = total + jnp.dot(
                gall[row].reshape(tokens, block), tall[row, :, at], preferred_element_type=jnp.float32
            )
        hid_out[:, at] = total.astype(jnp.bfloat16)

    for group in (send_h, send_p, send_c, send_s, send_g, send_f):
        for copy in group.values():
            copy.wait_send()


def hand_out(hid, tab, hid_out, tab_out):
    hid_out[...] = hid[...]
    tab_out[...] = tab[...]


def shards(hidden, cotangent, table, token_ids, target_ids, row_counts):
    block, cols = table.shape
    rows = hidden.shape[0]
    tokens = token_ids.shape[0]
    vmem = pl.BlockSpec(memory_space=pltpu.VMEM)
    hbm = pl.BlockSpec(memory_space=pl.ANY)
    dma = pltpu.SemaphoreType.DMA
    results = pl.pallas_call(
        kernel,
        out_shape=(
            jax.ShapeDtypeStruct((tokens, cols), jnp.bfloat16),
            jax.ShapeDtypeStruct((block, cols), jnp.bfloat16),
        ),
        in_specs=[hbm, hbm, hbm, vmem, vmem, pl.BlockSpec(memory_space=pltpu.SMEM)],
        out_specs=(vmem, vmem),
        scratch_shapes=[
            pltpu.VMEM((4, block, cols), jnp.bfloat16),
            pltpu.VMEM((4, rows, cols), jnp.bfloat16),
            pltpu.VMEM((4, rows, cols), jnp.bfloat16),
            pltpu.VMEM((4, rows, block), jnp.float32),
            pltpu.VMEM((4, rows, block), jnp.float32),
            pltpu.VMEM((4, 8, 128), jnp.float32),
            pltpu.VMEM((4, 4, rows, block), jnp.bfloat16),
            pltpu.VMEM((tokens, 128), jnp.float32),
            dma((3,)),
            *[dma((4,))] * 4,
            *[dma((16,))] * 4,
            *[dma((4,))] * 6,
            dma((4, 4)),
            dma((4, 4)),
        ],
        compiler_params=pltpu.CompilerParams(
            collective_id=0, has_side_effects=True, vmem_limit_bytes=60 * 1024 * 1024
        ),
        cost_estimate=pl.CostEstimate(flops=1200000000, bytes_accessed=6000000, transcendentals=40000),
    )(hidden, cotangent, table, token_ids[None, :], target_ids[None, :], row_counts)
    return pl.pallas_call(
        hand_out,
        out_shape=tuple(jax.ShapeDtypeStruct(a.shape, a.dtype) for a in results),
        grid=(2,),
        in_specs=[pl.BlockSpec((a.shape[0] // 2, cols), lambda i: (i, 0)) for a in results],
        out_specs=tuple(pl.BlockSpec((a.shape[0] // 2, cols), lambda i: (i, 0)) for a in results),
    )(*results)


def solution(mesh):
    sizes = tuple(mesh.shape[axis] for axis in ("groups", "vocab", "dp", "rep"))

    def part(hidden, cotangent, table, token_ids, target_ids, row_counts):
        block, cols = table.shape
        fits = (
            sizes == (2, 4, 2, 2)
            and hidden.shape[0] == ROW_LEN
            and cols % TILE == 0
            and block == 256
            and token_ids.shape[0] == 256
        )
        run = shards if fits else plain
        return run(hidden, cotangent, table, token_ids, target_ids, row_counts)

    in_specs = (
        P(("groups", "dp", "rep"), None),
        P(("groups", "dp", "rep"), None),
        P("vocab", ("dp", "rep")),
        P("groups"),
        P("groups"),
        P("groups"),
    )
    out_specs = (P("groups", ("dp", "rep")), P(("groups", "vocab"), ("dp", "rep")))
    return jax.shard_map(part, mesh=mesh, in_specs=in_specs, out_specs=out_specs, check_vma=False)
```
